256 devices in a mesh: section: 32 (over z_hi, x, core), rep: 8 (over z_lo, y).
Axes of the slice: x: 4, y: 4, z: 8 (z_hi: 4, z_lo: 2; z = z_hi * 2 + z_lo), core: 2. Of those that a mesh axis runs over, the one named last changes fastest.
Arguments:
- features: bfloat16 [65536, 128], P(('section', 'rep')), may hold values from -6 to 6
- weight: bfloat16 [128, 256], replicated, may hold values from -0.5 to 0.5
- bias: float32 [256], replicated, may hold values from -3 to 3
- tile_vals: bfloat16 [32, 32, 16, 6, 128, 128], P('section', 'rep'), may hold values from -0.15625 to 0.15625
- tile_cols: int32 [32, 32, 16, 6], P('section', 'rep'), may hold values from 0 to 15
- tile_counts: int32 [32, 32, 16], P('section', 'rep'), may hold values from 0 to 6, as said below
Outputs:
- hidden_out: bfloat16 [65536, 256], P(('section', 'rep'))
The draws below stay inside these ranges and needn't reach their ends.
Inputs may be any that keep to these rules, and one draw needn't show every extreme that they name: `tile_counts`: most tile rows have no live slot for a given source block; each block pair i, j has a tile row with exactly 6 live slots.
All inputs are finite; a program needn't handle non-finite values.
Results may differ from the reference program's by a relative error of at most 0.0047.
Values may be sent and summed in bfloat16 or wider, within the bound.
No kernel may reach another device: no remote copies, remote signals or barrier semaphores. Data moves between devices by JAX's collectives and lax.ppermute only.
A program may use at most 128 MiB of HBM per device.

```python
import jax
import jax.numpy as jnp
from jax import lax

TILE = 128
FEAT = 128
HID = 256
TROWS = 16
PER_ROW = 6
NODES = 65536
N_SECTION = 32


def lax_iota(shape, dim):
    return jax.lax.broadcasted_iota(jnp.int32, shape, dim)


def draw_tile_counts(key, part):
    shape = (N_SECTION, N_SECTION, TROWS)
    base = jax.random.randint(jax.random.fold_in(key, 1), shape, 1, PER_ROW + 1, dtype=jnp.int32)
    keep = jax.random.randint(jax.random.fold_in(key, 2), shape, 0, 8, dtype=jnp.int32) == 0
    first = lax_iota(shape, 0)
    second = lax_iota(shape, 1)
    third = lax_iota(shape, 2)
    full = third == (first + second) % TROWS
    sparse = jnp.where(keep, base, jnp.zeros(shape, jnp.int32))
    return jnp.where(full, jnp.int32(PER_ROW), sparse)


def with_ends(array, key, smallest, largest):
    shape = array.shape
    spot = [jax.random.randint(jax.random.fold_in(key, axis), (), 0, shape[axis]) for axis in range(len(shape))]
    array = array.at[tuple(spot)].set(smallest)
    longest = shape.index(max(shape))
    spot[longest] = (spot[longest] + 1) % shape[longest]
    return array.at[tuple(spot)].set(largest)


def steps_of(key, extent, shards, low, largest):
    def one(position, blocks):
        draws = jax.random.uniform(jax.random.fold_in(jax.random.fold_in(key, 6), position), (blocks,), jnp.float32, low / len(shards), largest / len(shards))
        return jnp.repeat(jnp.exp(draws), extent[position] // blocks).reshape((-1,) + (1,) * (len(extent) - position - 1))

    gain = one(*shards[0])
    for cut in shards[1:]:
        gain = gain * one(*cut)
    return gain


def normal_values(stream_key, extent, width, limit, cuts=(), kind=jnp.bfloat16):
    values = jax.random.normal(stream_key, extent, jnp.float32) * width
    if len(cuts) > 0:
        values = steps_of(stream_key, extent, cuts, -0.22, 0.18) * values
    return jnp.clip(values, min=-limit, max=limit).astype(kind)


def setup_inputs(seed: int = 0) -> dict:
    streams_of = jax.random.split(jax.random.key(seed), 7)
    features = normal_values(streams_of[0], (NODES, FEAT), 1.0, 6.0, ((0, 256),))
    weight = normal_values(streams_of[1], (FEAT, HID), FEAT ** -0.5, 0.5)
    bias = normal_values(streams_of[2], (HID,), 0.5, 3.0, (), jnp.float32)
    tile_vals = normal_values(streams_of[3], (N_SECTION, N_SECTION, TROWS, PER_ROW, TILE, TILE), (TILE * PER_ROW * 2) ** -0.5, 0.15625, ((0, 32), (1, 8)))
    tile_cols = with_ends(jax.random.randint(streams_of[4], (N_SECTION, N_SECTION, TROWS, PER_ROW), 0, TROWS), jax.random.fold_in(streams_of[4], 1), 0, TROWS - 1).astype(jnp.int32)
    tile_counts = draw_tile_counts(jax.random.fold_in(streams_of[6], 71), 0)
    return dict(features=features, weight=weight, bias=bias, tile_vals=tile_vals, tile_cols=tile_cols, tile_counts=tile_counts)


def reference(features, weight, bias, tile_vals, tile_cols, tile_counts):
    product = jnp.dot(features, weight, preferred_element_type=jnp.float32).astype(jnp.bfloat16)
    sections = tile_vals.shape[0]
    trows = tile_vals.shape[2]
    per_row = tile_vals.shape[3]
    tile = tile_vals.shape[4]
    hidden = weight.shape[1]
    blocks = product.reshape(sections, trows, tile, hidden)

    def one_target(inputs):
        values, columns, counts = inputs

        def add_source(total, source):
            block, tile_block, col_block, count_block = source
            picked = jnp.take(block, col_block, axis=0)
            live = jnp.arange(per_row, dtype=jnp.int32)[None, :] < count_block[:, None]
            picked = jnp.where(live[:, :, None, None], picked, jnp.zeros((), picked.dtype))
            term = jnp.einsum("tpab,tpbh->tah", tile_block.astype(jnp.float32), picked.astype(jnp.float32))
            return total + term, None

        start = jnp.zeros((trows, tile, hidden), jnp.float32)
        total, _ = lax.scan(add_source, start, (blocks, values, columns, counts))
        return total

    summed = lax.map(one_target, (tile_vals, tile_cols, tile_counts))
    summed = summed.reshape(sections * trows * tile, hidden)
    return jnp.maximum(summed + bias, 0.0).astype(jnp.bfloat16)
```

```python
import functools

import jax
import jax.numpy as jnp
import numpy as np
from jax import lax
from jax.experimental import pallas as pl
from jax.experimental.pallas import tpu as pltpu
from jax.sharding import PartitionSpec as P

SECTIONS, REPS, CHUNKS = 32, 8, 32
TILE = 128
GROUP = 8


def section_of(z, x, core):
    return z * 8 + x * 2 + core


def landing(block, replica):
    z, x, core = block // 8, block // 2 % 4, block % 2
    half, y = replica // 4, replica % 4
    owner = block // 4
    away = (y - owner % 4) % 4
    beside = (x + 1 if x % 2 else x - 1) % 4
    if half == owner // 4:
        up, moves = {2: (0, 0), 1: (0, 1), 3: (1, 0), 0: (1, 1)}[away]
        if half == 0:
            up = -up
    else:
        up, moves = {2: (1, 0), 1: (1, 1), 3: (2, 0), 0: (2, 1)}[away]
        if half == 0:
            up = {1: -1, 2: 2}[up]
    return section_of((z + up) % 4, beside if moves else x, core), owner


def swaps(axis, step):
    pairs = []
    for s in range(SECTIONS):
        z, x, core = s // 8, s // 2 % 4, s % 2
        at = z if axis == "z" else x
        if (step + core) % 2 == 0:
            to = at ^ 1
        else:
            to = (at + 1) % 4 if at % 2 else (at - 1) % 4
        pairs.append((s, section_of(to, x, core) if axis == "z" else section_of(z, to, core)))
    return pairs


LAND = []
for _b in range(SECTIONS):
    for _r in range(REPS):
        _s, _o = landing(_b, _r)
        LAND.append((_b * REPS + _r, _s * REPS + _o))
CORES = [(s, s ^ 1) for s in range(SECTIONS)]
STEPS = [swaps("z", 0), swaps("z", 1), swaps("x", 0), swaps("x", 1)]


def chunk_slots():
    held = [None] * (SECTIONS * REPS)
    for source, target in LAND:
        held[target] = [source]
    for pairs in STEPS + [CORES]:
        before = [list(h) for h in held]
        for s, t in pairs:
            for r in range(REPS):
                held[t * REPS + r] = before[t * REPS + r] + before[s * REPS + r]
    table = np.zeros((SECTIONS * REPS, CHUNKS), np.int32)
    for device in range(SECTIONS * REPS):
        replica = device % REPS
        for place, chunk in enumerate(held[device]):
            table[device, chunk - replica * CHUNKS] = place
        assert sorted(table[device]) == list(range(CHUNKS))
    return table


SLOTS = chunk_slots()


def list_kernel(per_row, counts, cols, slots, entries, number):
    rows = counts.shape[0]
    trows = rows // 4

    def add(row, done):
        live = counts[row]
        block = row // trows

        def one(p, carry):
            tile = row * per_row + p
            col = cols[tile]
            place = slots[block * 8 + col // 2] * 2 + col % 2
            entries[done + p] = tile + place * 512 + (row % trows) * 65536
            return carry

        lax.fori_loop(0, live, one, 0)
        return done + live

    total = lax.fori_loop(0, rows, add, 0)
    number[0] = (total + GROUP - 1) // GROUP
    for extra in range(GROUP):
        entries[total + extra] = 2 * CHUNKS * 512


def tiles_kernel(entries, number, vals, x0, x1, x2, x3, out, xs, acc):
    rows = x0.shape[0]
    for k, piece in enumerate((x0, x1, x2, x3)):
        xs[k * rows : (k + 1) * rows, :] = piece[...]
    xs[4 * rows :, :] = jnp.zeros((TILE, TILE), xs.dtype)
    acc[...] = jnp.zeros_like(acc)

    def step(g, carry):
        products = []
        for k in range(GROUP):
            entry = entries[g * GROUP + k]
            place = pl.multiple_of((entry // 512 % 128) * TILE, TILE)
            products.append(
                (
                    pl.multiple_of(entry // 65536 * TILE, TILE),
                    jnp.dot(vals[entry % 512], xs[pl.ds(place, TILE), :], preferred_element_type=jnp.float32),
                )
            )
        for at, product in products:
            acc[pl.ds(at, TILE), :] += product
        return carry

    lax.fori_loop(0, number[0], step, 0)
    out[...] = acc[...].astype(out.dtype)


def finish_kernel(parts, weight, bias, out):
    total = parts[0].astype(jnp.float32)
    for k in range(1, REPS):
        total = total + parts[k].astype(jnp.float32)
    high = total.astype(jnp.bfloat16)
    low = (total - high.astype(jnp.float32)).astype(jnp.bfloat16)
    hidden = jnp.dot(high, weight[...], preferred_element_type=jnp.float32)
    hidden = hidden + jnp.dot(low, weight[...], preferred_element_type=jnp.float32)
    out[...] = jnp.maximum(hidden + bias[...], 0.0).astype(out.dtype)


SMEM = pl.BlockSpec(memory_space=pltpu.SMEM)
VMEM = pl.BlockSpec(memory_space=pltpu.VMEM)


def body(features, weight, bias, tile_vals, tile_cols, tile_counts):
    _, blocks, trows, per_row, tile, _ = tile_vals.shape
    tiles = blocks * trows * per_row
    feat = features.shape[1]
    device = lax.axis_index("section") * REPS + lax.axis_index("rep")
    slots = lax.dynamic_slice(jnp.asarray(SLOTS), (device, 0), (1, CHUNKS)).reshape(CHUNKS)

    entries, number = pl.pallas_call(
        functools.partial(list_kernel, per_row),
        out_shape=(
            jax.ShapeDtypeStruct((tiles + GROUP,), jnp.int32),
            jax.ShapeDtypeStruct((1,), jnp.int32),
        ),
        in_specs=[SMEM] * 3,
        out_specs=(SMEM, SMEM),
        cost_estimate=pl.CostEstimate(flops=4000, bytes_accessed=4096, transcendentals=0),
        name="list_live_tiles",
    )(tile_counts.reshape(-1), tile_cols.reshape(-1), slots)

    held = lax.ppermute(features, ("section", "rep"), LAND)
    for pairs in STEPS[:-1]:
        held = jnp.concatenate([held, lax.ppermute(held, "section", pairs)], 0)
    last = lax.ppermute(held, "section", STEPS[-1])
    pieces = (held, last, lax.ppermute(held, "section", CORES), lax.ppermute(last, "section", CORES))

    partial_sums = pl.pallas_call(
        tiles_kernel,
        out_shape=jax.ShapeDtypeStruct((trows * tile, feat), jnp.bfloat16),
        in_specs=[SMEM] * 2 + [VMEM] * 5,
        out_specs=VMEM,
        scratch_shapes=[
            pltpu.VMEM((CHUNKS * features.shape[0] + TILE, feat), jnp.bfloat16),
            pltpu.VMEM((trows * tile, feat), jnp.float32),
        ],
        compiler_params=pltpu.CompilerParams(vmem_limit_bytes=40 * 2**20),
        cost_estimate=pl.CostEstimate(flops=2 * 60 * tile * tile * feat, bytes_accessed=8 * 2**20, transcendentals=0),
        name="sum_live_tiles",
    )(entries, number, tile_vals.reshape(tiles, tile, tile), *pieces)

    parts = lax.all_to_all(partial_sums, "rep", 0, 0, tiled=True)
    own = features.shape[0]
    return pl.pallas_call(
        finish_kernel,
        out_shape=jax.ShapeDtypeStruct((own, weight.shape[1]), jnp.bfloat16),
        in_specs=[VMEM] * 3,
        out_specs=VMEM,
        cost_estimate=pl.CostEstimate(flops=4 * own * feat * weight.shape[1], bytes_accessed=2**20, transcendentals=0),
        name="apply_weight",
    )(parts.reshape(REPS, own, feat), weight, bias.reshape(1, -1))


def solution(mesh):
    placed = (
        P(("section", "rep"), None),
        P(),
        P(),
        P("section", "rep", None, None, None, None),
        P("section", "rep", None, None),
        P("section", "rep", None),
    )
    return jax.shard_map(
        body, mesh=mesh, in_specs=placed, out_specs=P(("section", "rep"), None), check_vma=False
    )
```

```python
import functools

import jax
import jax.numpy as jnp
import numpy as np
from jax import lax
from jax.experimental import pallas as pl
from jax.experimental.pallas import tpu as pltpu
from jax.sharding import PartitionSpec as P

SECTIONS, REPS, CHUNKS = 32, 8, 32
TILE = 128
EARLY = 16
GROUP = 8


def section_of(z, x, core):
    return z * 8 + x * 2 + core


def landing(block, replica):
    z, x, core = block // 8, block // 2 % 4, block % 2
    half, y = replica // 4, replica % 4
    owner = block // 4
    away = (y - owner % 4) % 4
    beside = (x + 1 if x % 2 else x - 1) % 4
    if half == owner // 4:
        up, moves = {2: (0, 0), 1: (0, 1), 3: (1, 0), 0: (1, 1)}[away]
        if half == 0:
            up = -up
    else:
        up, moves = {2: (1, 0), 1: (1, 1), 3: (2, 0), 0: (2, 1)}[away]
        if half == 0:
            up = {1: -1, 2: 2}[up]
    return section_of((z + up) % 4, beside if moves else x, core), owner


def swaps(axis, step):
    pairs = []
    for s in range(SECTIONS):
        z, x, core = s // 8, s // 2 % 4, s % 2
        at = z if axis == "z" else x
        if (step + core) % 2 == 0:
            to = at ^ 1
        else:
            to = (at + 1) % 4 if at % 2 else (at - 1) % 4
        pairs.append((s, section_of(to, x, core) if axis == "z" else section_of(z, to, core)))
    return pairs


LAND = []
for _b in range(SECTIONS):
    for _r in range(REPS):
        _s, _o = landing(_b, _r)
        LAND.append((_b * REPS + _r, _s * REPS + _o))
CORES = [(s, s ^ 1) for s in range(SECTIONS)]
Z_SWAPS = [swaps("z", 0), swaps("z", 1)]
X_SWAPS = [swaps("x", 0), swaps("x", 1)]


def chunk_slots():
    def swap(held, pairs):
        got = [None] * len(held)
        for s, t in pairs:
            for r in range(REPS):
                got[t * REPS + r] = held[s * REPS + r]
        return got

    def ring(held, pairs):
        first, second = swap(held, pairs[0]), swap(held, pairs[1])
        return [held, first, second, swap(first, pairs[1])]

    def joined(pieces):
        return [sum(p, []) for p in zip(*pieces)]

    held = [None] * (SECTIONS * REPS)
    for source, target in LAND:
        held[target] = [source]
    pieces = ring(joined(ring(held, Z_SWAPS)), X_SWAPS)
    held = joined(pieces + [swap(p, CORES) for p in pieces])
    table = np.zeros((SECTIONS * REPS, CHUNKS, 2), np.int32)
    for device in range(SECTIONS * REPS):
        replica = device % REPS
        for place, chunk in enumerate(held[device]):
            table[device, chunk - replica * CHUNKS] = 2 * place, 2 * place + 1
        assert sorted(table[device].ravel()) == list(range(2 * CHUNKS))
    return table.reshape(SECTIONS * REPS, 2 * CHUNKS)


SLOTS = chunk_slots()


def prepare_kernel(slots, counts_hbm, cols_hbm, tile_vals, entries, vals, counts, cols, small_sem, sem):
    small = [
        pltpu.make_async_copy(counts_hbm, counts, small_sem.at[0]),
        pltpu.make_async_copy(cols_hbm, cols, small_sem.at[1]),
    ]
    for copy in small:
        copy.start()
    for copy in small:
        copy.wait()
    _, blocks, trows = counts.shape
    per_row = cols.shape[1]
    room = blocks * trows * per_row + GROUP

    def row_copy(row):
        part = pl.ds(row * per_row, per_row)
        return pltpu.make_async_copy(tile_vals.at[part], vals.at[part], sem.at[row])

    first = second = jnp.int32(0)
    for row in range(blocks * trows):
        block, trow = row // trows, row % trows
        live = counts[0, block, trow]
        pl.when(live > 0)(row_copy(row).start)

        def one(p, done, row=row, block=block, trow=trow):
            first, second = done
            place = slots[0, block * trows + cols[0, p, block, trow]]
            entry = place * 512 + (p + (row * per_row + trow * 65536))
            entries[first] = entry
            entries[room + second] = entry
            is_early = jnp.where(place < EARLY, 1, 0)
            return first + is_early, second + 1 - is_early

        first, second = lax.fori_loop(0, live, one, (first, second))
    for start, end in ((0, first), (room, second)):
        spare = entries[start + jnp.maximum(end - 1, 0)] % 512 + 2 * CHUNKS * 512
        for extra in range(GROUP):
            entries[start + end + extra] = spare
    entries[2 * room] = (first + GROUP - 1) // GROUP
    entries[2 * room + 1] = (second + GROUP - 1) // GROUP
    for row in range(blocks * trows):
        pl.when(counts[0, row // trows, row % trows] > 0)(row_copy(row).wait)


def add_tiles(entries, start, groups, vals, xs, acc):
    def step(g, carry):
        products = []
        for k in range(GROUP):
            entry = entries[start + g * GROUP + k]
            place = pl.multiple_of((entry // 512 % 128) * TILE, TILE)
            products.append(
                (
                    pl.multiple_of(entry // 65536 * TILE, TILE),
                    jnp.dot(vals[entry % 512], xs[pl.ds(place, TILE), :], preferred_element_type=jnp.float32),
                )
            )
        for at, product in products:
            acc[pl.ds(at, TILE), :] += product
        return carry

    lax.fori_loop(0, groups, step, 0)


def place_rows(xs, first, pieces):
    rows = pieces[0].shape[0]
    for k, piece in enumerate(pieces):
        xs[(first + k) * rows : (first + k + 1) * rows, :] = piece[...]
    xs[CHUNKS * 2 * TILE :, :] = jnp.zeros((TILE, xs.shape[1]), xs.dtype)


def early_kernel(entries, vals, *refs):
    *pieces, acc, xs = refs
    room = vals.shape[0] + GROUP
    place_rows(xs, 0, pieces)
    acc[...] = jnp.zeros_like(acc)
    add_tiles(entries, 0, entries[2 * room], vals, xs, acc)


def late_kernel(entries, vals, acc, *refs):
    *pieces, out, total, xs = refs
    room = vals.shape[0] + GROUP
    place_rows(xs, 2, pieces)
    total[...] = acc[...]
    add_tiles(entries, room, entries[2 * room + 1], vals, xs, total)
    out[...] = total[...].astype(out.dtype)


def finish_kernel(parts, weight, bias, out):
    total = parts[0].astype(jnp.float32)
    for k in range(1, REPS):
        total = total + parts[k].astype(jnp.float32)
    high = total.astype(jnp.bfloat16)
    low = (total - high.astype(jnp.float32)).astype(jnp.bfloat16)
    hidden = jnp.dot(high, weight[...], preferred_element_type=jnp.float32)
    hidden = hidden + jnp.dot(low, weight[...], preferred_element_type=jnp.float32)
    out[...] = jnp.maximum(hidden + bias[...], 0.0).astype(out.dtype)


SMEM = pl.BlockSpec(memory_space=pltpu.SMEM)
VMEM = pl.BlockSpec(memory_space=pltpu.VMEM)
HBM = pl.BlockSpec(memory_space=pltpu.HBM)


def estimate(flops, moved):
    return pl.CostEstimate(flops=flops, bytes_accessed=moved, transcendentals=0)


def body(features, weight, bias, tile_vals, tile_cols, tile_counts):
    _, blocks, trows, per_row, tile, _ = tile_vals.shape
    tiles = blocks * trows * per_row
    own, feat = features.shape
    device = lax.axis_index("section") * REPS + lax.axis_index("rep")
    gathered = CHUNKS * own + TILE

    def swap(array, pairs):
        return lax.ppermute(array, "section", pairs)

    def ring(array, pairs):
        first, second = swap(array, pairs[0]), swap(array, pairs[1])
        return jnp.concatenate([array, first, second, swap(first, pairs[1])], 0)

    mine = lax.ppermute(features, ("section", "rep"), LAND)
    slots = lax.dynamic_slice(jnp.asarray(SLOTS), (device, 0), (1, 2 * CHUNKS))
    mine, slots = lax.optimization_barrier((mine, slots))
    mine = ring(mine, Z_SWAPS)
    mine, vals, cols, counts, slots = lax.optimization_barrier(
        (mine, tile_vals.reshape(tiles, tile, tile), tile_cols.transpose(0, 3, 1, 2), tile_counts, slots)
    )

    first = swap(mine, X_SWAPS[0])
    second = swap(mine, X_SWAPS[1])
    entries, vals = pl.pallas_call(
        prepare_kernel,
        out_shape=(
            jax.ShapeDtypeStruct((2 * (tiles + GROUP) + 2,), jnp.int32),
            jax.ShapeDtypeStruct(vals.shape, vals.dtype),
        ),
        in_specs=[SMEM] + [HBM] * 3,
        out_specs=(SMEM, VMEM),
        scratch_shapes=[
            pltpu.SMEM(counts.shape, jnp.int32),
            pltpu.SMEM(cols.shape, jnp.int32),
            pltpu.SemaphoreType.DMA((2,)),
            pltpu.SemaphoreType.DMA((blocks * trows,)),
        ],
        compiler_params=pltpu.CompilerParams(vmem_limit_bytes=40 * 2**20),
        cost_estimate=estimate(4000, 4 * vals.size),
        name="list_live_tiles",
    )(slots, counts, cols, vals)
    first, entries, vals = lax.optimization_barrier((first, entries, vals))

    third = swap(first, X_SWAPS[1])
    beside = [swap(piece, CORES) for piece in (mine, first, second)]
    acc = pl.pallas_call(
        early_kernel,
        out_shape=jax.ShapeDtypeStruct((trows * tile, feat), jnp.float32),
        in_specs=[SMEM] + [VMEM] * 3,
        out_specs=VMEM,
        scratch_shapes=[pltpu.VMEM((gathered, feat), jnp.bfloat16)],
        compiler_params=pltpu.CompilerParams(vmem_limit_bytes=24 * 2**20),
        cost_estimate=estimate(2 * 15 * tile * tile * feat, 2**20),
        name="sum_early_tiles",
    )(entries, vals, mine, first)
    third, acc = lax.optimization_barrier((third, acc))

    partial_sums = pl.pallas_call(
        late_kernel,
        out_shape=jax.ShapeDtypeStruct((trows * tile, feat), jnp.bfloat16),
        in_specs=[SMEM] + [VMEM] * 8,
        out_specs=VMEM,
        scratch_shapes=[
            pltpu.VMEM((trows * tile, feat), jnp.float32),
            pltpu.VMEM((gathered, feat), jnp.bfloat16),
        ],
        compiler_params=pltpu.CompilerParams(vmem_limit_bytes=24 * 2**20),
        cost_estimate=estimate(2 * 45 * tile * tile * feat, 2**20),
        name="sum_late_tiles",
    )(entries, vals, acc, second, third, *beside, swap(third, CORES))

    parts = lax.all_to_all(partial_sums, "rep", 0, 0, tiled=True)
    return pl.pallas_call(
        finish_kernel,
        out_shape=jax.ShapeDtypeStruct((own, weight.shape[1]), jnp.bfloat16),
        in_specs=[VMEM] * 3,
        out_specs=VMEM,
        cost_estimate=estimate(4 * own * feat * weight.shape[1], 2**20),
        name="apply_weight",
    )(parts.reshape(REPS, own, feat), weight, bias.reshape(1, -1))


def solution(mesh):
    placed = (
        P(("section", "rep"), None),
        P(),
        P(),
        P("section", "rep", None, None, None, None),
        P("section", "rep", None, None),
        P("section", "rep", None),
    )
    return jax.shard_map(
        body, mesh=mesh, in_specs=placed, out_specs=P(("section", "rep"), None), check_vma=False
    )
```

```python
import functools

import jax
import jax.numpy as jnp
import numpy as np
from jax import lax
from jax.experimental import pallas as pl
from jax.experimental.pallas import tpu as pltpu
from jax.sharding import PartitionSpec as P

SECTIONS, REPS, CHUNKS = 32, 8, 32
TILE = 128
STAGES = (24, 56, 64)
GROUP = 8


def section_of(z, x, core):
    return z * 8 + x * 2 + core


def partner(at, odd):
    return (at + 1 - 2 * (at % 2)) % 4 if not odd else (at - 1 + 2 * (at % 2)) % 4


def landings(block, replica):
    z, x, core = block // 8, block // 2 % 4, block % 2
    owner = block // 4
    away = (replica % 4 - owner % 4) % 4
    beside = (x + 1 if x % 2 else x - 1) % 4
    near = [z, partner(z, core)]
    if replica // 4 != owner // 4:
        near = [p for p in range(4) if p not in near]
    if away % 3 == 0:
        x = beside
    if away % 2:
        near.reverse()
    if away == 3:
        near.reverse()
    if away == 0:
        near.reverse()
    planes = near + [partner(p, 1 - core) for p in near]
    return [section_of(p, x, core) for p in planes], owner


def swaps(step):
    pairs = []
    for s in range(SECTIONS):
        z, x, core = s // 8, s // 2 % 4, s % 2
        pairs.append((s, section_of(z, partner(x, (step + core) % 2), core)))
    return pairs


LANDS = [[], [], [], []]
for _b in range(SECTIONS):
    for _r in range(REPS):
        _places, _o = landings(_b, _r)
        for _pairs, _s in zip(LANDS, _places):
            _pairs.append((_b * REPS + _r, _s * REPS + _o))
CORES = [(s, s ^ 1) for s in range(SECTIONS)]
X_SWAPS = [swaps(0), swaps(1)]


def chunk_slots():
    def swap(held, pairs):
        got = [None] * len(held)
        for s, t in pairs:
            for r in range(REPS):
                got[t * REPS + r] = held[s * REPS + r]
        return got

    def ring(held, pairs):
        first, second = swap(held, pairs[0]), swap(held, pairs[1])
        return [held, first, second, swap(first, pairs[1])]

    def joined(pieces):
        return [sum(p, []) for p in zip(*pieces)]

    held = [[] for _ in range(SECTIONS * REPS)]
    for pairs in LANDS:
        for source, target in pairs:
            held[target].append(source)
    pieces = ring(held, X_SWAPS)
    held = joined(pieces + [swap(p, CORES) for p in pieces])
    table = np.zeros((SECTIONS * REPS, CHUNKS, 2), np.int32)
    for device in range(SECTIONS * REPS):
        replica = device % REPS
        for place, chunk in enumerate(held[device]):
            table[device, chunk - replica * CHUNKS] = 2 * place, 2 * place + 1
        assert sorted(table[device].ravel()) == list(range(2 * CHUNKS))
    return table.reshape(SECTIONS * REPS, 4, 2 * CHUNKS // 4)


SLOTS = chunk_slots()


def prepare_kernel(small, tile_vals, entries, vals, sem):
    _, blocks, trows = small.shape
    per_row = small.shape[0] - 2
    room = blocks * trows * per_row + GROUP

    def row_copy(row):
        part = pl.ds(row * per_row, per_row)
        return pltpu.make_async_copy(tile_vals.at[part], vals.at[part], sem.at[row])

    ends = (jnp.int32(0),) * len(STAGES)
    for row in range(blocks * trows):
        block, trow = row // trows, row % trows
        live = small[1, block, trow]

        def one(p, ends, row=row, block=block, trow=trow):
            place = small[0, block, small[2 + p, block, trow]]
            entry = place * 512 + (p + (row * per_row + trow * 65536))
            for stage, end in enumerate(ends):
                entries[stage * room + end] = entry
            within = [jnp.where(place < limit, 1, 0) for limit in STAGES[:-1]] + [1]
            return tuple(end + w - v for end, w, v in zip(ends, within, [0] + within[:-1]))

        def some(ends, row=row, live=live, one=one):
            row_copy(row).start()
            return lax.fori_loop(0, live, one, ends)

        ends = lax.cond(live > 0, some, lambda ends: ends, ends)
    for stage, end in enumerate(ends):
        spare = entries[stage * room + jnp.maximum(end - 1, 0)] % 512 + 2 * CHUNKS * 512
        for extra in range(GROUP):
            entries[stage * room + end + extra] = spare
        entries[len(STAGES) * room + stage] = (end + GROUP - 1) // GROUP
    for row in range(blocks * trows):
        pl.when(small[1, row // trows, row % trows] > 0)(row_copy(row).wait)


def stage_kernel(stage, entries, vals, *refs):
    last = stage == len(STAGES) - 1
    *pieces, out, xs, total = refs if last else refs + (refs[-2],)
    before = pieces.pop(0) if stage else None
    base = STAGES[stage - 1] if stage else 0
    room = vals.shape[0] + GROUP
    rows = 0
    for piece in pieces:
        xs[rows : rows + piece.shape[0], :] = piece[...]
        rows += piece.shape[0]
    xs[rows:, :] = jnp.zeros((TILE, xs.shape[1]), xs.dtype)
    total[...] = jnp.zeros_like(total) if before is None else before[...]

    def step(g, carry):
        products = []
        for k in range(GROUP):
            entry = entries[stage * room + g * GROUP + k]
            place = jnp.minimum(entry // 512 % 128 - base, rows // TILE)
            products.append(
                (
                    pl.multiple_of(entry // 65536 * TILE, TILE),
                    jnp.dot(
                        vals[entry % 512],
                        xs[pl.ds(pl.multiple_of(place * TILE, TILE), TILE), :],
                        preferred_element_type=jnp.float32,
                    ),
                )
            )
        for at, product in products:
            total[pl.ds(at, TILE), :] += product
        return carry

    lax.fori_loop(0, entries[len(STAGES) * room + stage], step, 0)
    if last:
        out[...] = total[...].astype(out.dtype)


def finish_kernel(parts, weight, bias, out):
    total = parts[0].astype(jnp.float32)
    for k in range(1, REPS):
        total = total + parts[k].astype(jnp.float32)
    high = total.astype(jnp.bfloat16)
    low = (total - high.astype(jnp.float32)).astype(jnp.bfloat16)
    hidden = jnp.dot(high, weight[...], preferred_element_type=jnp.float32)
    hidden = hidden + jnp.dot(low, weight[...], preferred_element_type=jnp.float32)
    out[...] = jnp.maximum(hidden + bias[...], 0.0).astype(out.dtype)


SMEM = pl.BlockSpec(memory_space=pltpu.SMEM)
VMEM = pl.BlockSpec(memory_space=pltpu.VMEM)
HBM = pl.BlockSpec(memory_space=pltpu.HBM)


def estimate(flops, moved):
    return pl.CostEstimate(flops=flops, bytes_accessed=moved, transcendentals=0)


def body(features, weight, bias, tile_vals, tile_cols, tile_counts):
    _, blocks, trows, per_row, tile, _ = tile_vals.shape
    tiles = blocks * trows * per_row
    own, feat = features.shape
    device = lax.axis_index("section") * REPS + lax.axis_index("rep")

    def swap(array, pairs):
        return lax.ppermute(array, "section", pairs)

    small = jnp.concatenate(
        [
            lax.dynamic_slice(jnp.asarray(SLOTS), (device, 0, 0), (1, blocks, trows)),
            tile_counts,
            tile_cols[0].transpose(2, 0, 1),
        ],
        0,
    )
    landed = [lax.ppermute(features, ("section", "rep"), pairs) for pairs in LANDS]
    entries, vals = pl.pallas_call(
        prepare_kernel,
        out_shape=(
            jax.ShapeDtypeStruct((len(STAGES) * (tiles + GROUP + 1),), jnp.int32),
            jax.ShapeDtypeStruct((tiles, tile, tile), tile_vals.dtype),
        ),
        in_specs=[SMEM, HBM],
        out_specs=(SMEM, VMEM),
        scratch_shapes=[
            pltpu.SemaphoreType.DMA((blocks * trows,)),
        ],
        compiler_params=pltpu.CompilerParams(vmem_limit_bytes=40 * 2**20),
        cost_estimate=estimate(4000, 4 * tile_vals.size),
        name="list_live_tiles",
    )(small, tile_vals.reshape(tiles, tile, tile))
    mine = jnp.concatenate(landed, 0)
    mine, entries, vals = lax.optimization_barrier((mine, entries, vals))

    first = swap(mine, X_SWAPS[0])
    second = swap(mine, X_SWAPS[1])
    third = swap(first, X_SWAPS[1])
    beside = [swap(piece, CORES) for piece in (mine, first, second)]
    def add_stage(stage, before, pieces):
        rows = sum(piece.shape[0] for piece in pieces)
        last = stage == len(STAGES) - 1
        ins = ([before] if stage else []) + list(pieces)
        scratch = [pltpu.VMEM((rows + TILE, feat), jnp.bfloat16)]
        if last:
            scratch.append(pltpu.VMEM((trows * tile, feat), jnp.float32))
        return pl.pallas_call(
            functools.partial(stage_kernel, stage),
            out_shape=jax.ShapeDtypeStruct((trows * tile, feat), jnp.bfloat16 if last else jnp.float32),
            in_specs=[SMEM] + [VMEM] * (1 + len(ins)),
            out_specs=VMEM,
            scratch_shapes=scratch,
            compiler_params=pltpu.CompilerParams(vmem_limit_bytes=24 * 2**20),
            cost_estimate=estimate(2 * rows // 6 * tile * feat, 2**20),
            name=f"sum_stage_{stage}",
        )(entries, vals, *ins)

    acc = add_stage(0, None, (mine, first, second))
    third, acc = lax.optimization_barrier((third, acc))
    final = swap(third, CORES)
    acc = add_stage(1, acc, (third, *beside))
    final, acc = lax.optimization_barrier((final, acc))
    partial_sums = add_stage(2, acc, (final,))

    parts = lax.all_to_all(partial_sums, "rep", 0, 0, tiled=True)
    return pl.pallas_call(
        finish_kernel,
        out_shape=jax.ShapeDtypeStruct((own, weight.shape[1]), jnp.bfloat16),
        in_specs=[VMEM] * 3,
        out_specs=VMEM,
        compiler_params=pltpu.CompilerParams(vmem_limit_bytes=8 * 2**20),
        cost_estimate=estimate(4 * own * feat * weight.shape[1], 2**20),
        name="apply_weight",
    )(parts.reshape(REPS, own, feat), weight, bias.reshape(1, -1))


def solution(mesh):
    placed = (
        P(("section", "rep"), None),
        P(),
        P(),
        P("section", "rep", None, None, None, None),
        P("section", "rep", None, None),
        P("section", "rep", None),
    )
    return jax.shard_map(
        body, mesh=mesh, in_specs=placed, out_specs=P(("section", "rep"), None), check_vma=False
    )
```

```python
import functools

import jax
import jax.numpy as jnp
import numpy as np
from jax import lax
from jax.experimental import pallas as pl
from jax.experimental.pallas import tpu as pltpu
from jax.sharding import PartitionSpec as P

SECTIONS, REPS, CHUNKS = 32, 8, 32
TILE = 128
STAGES = (32, 56, 64)
GROUP = 8


def section_of(z, x, core):
    return z * 8 + x * 2 + core


def partner(at, odd):
    return (at + 1 - 2 * (at % 2)) % 4 if not odd else (at - 1 + 2 * (at % 2)) % 4


def landings(block, replica):
    z, x, core = block // 8, block // 2 % 4, block % 2
    owner = block // 4
    away = (replica % 4 - owner % 4) % 4
    beside = (x + 1 if x % 2 else x - 1) % 4
    near = [z, partner(z, core)]
    if replica // 4 != owner // 4:
        near = [p for p in range(4) if p not in near]
    if away % 3 == 0:
        x = beside
    if away % 2:
        near.reverse()
    if away == 3:
        near.reverse()
    if away == 0:
        near.reverse()
    planes = near + [partner(p, 1 - core) for p in near]
    return [section_of(p, x, core) for p in planes], owner


def swaps(step):
    pairs = []
    for s in range(SECTIONS):
        z, x, core = s // 8, s // 2 % 4, s % 2
        pairs.append((s, section_of(z, partner(x, (step + core) % 2), core)))
    return pairs


LANDS = [[], [], [], []]
for _b in range(SECTIONS):
    for _r in range(REPS):
        _places, _o = landings(_b, _r)
        for _pairs, _s in zip(LANDS, _places):
            _pairs.append((_b * REPS + _r, _s * REPS + _o))
CORES = [(s, s ^ 1) for s in range(SECTIONS)]
X_SWAPS = [swaps(0), swaps(1)]


def chunk_slots():
    def swap(held, pairs):
        got = [None] * len(held)
        for s, t in pairs:
            for r in range(REPS):
                got[t * REPS + r] = held[s * REPS + r]
        return got

    def ring(held, pairs):
        first, second = swap(held, pairs[0]), swap(held, pairs[1])
        return [held, first, second, swap(first, pairs[1])]

    def joined(pieces):
        return [sum(p, []) for p in zip(*pieces)]

    held = [[] for _ in range(SECTIONS * REPS)]
    for pairs in LANDS:
        for source, target in pairs:
            held[target].append(source)
    pieces = ring(held, X_SWAPS)
    beside = [swap(p, CORES) for p in pieces]
    held = joined(pieces[:3] + beside[:1] + pieces[3:] + beside[1:])
    table = np.zeros((SECTIONS * REPS, CHUNKS, 2), np.int32)
    for device in range(SECTIONS * REPS):
        replica = device % REPS
        for place, chunk in enumerate(held[device]):
            table[device, chunk - replica * CHUNKS] = 2 * place, 2 * place + 1
        assert sorted(table[device].ravel()) == list(range(2 * CHUNKS))
    return table.reshape(SECTIONS * REPS, 4, 2 * CHUNKS // 4)


SLOTS = chunk_slots()


def load_kernel(small, tile_vals, vals, sem):
    _, blocks, trows = small.shape
    per_row = small.shape[0] - 2

    def row_copy(row):
        part = pl.ds(row * per_row, per_row)
        return pltpu.make_async_copy(tile_vals.at[part], vals.at[part], sem.at[row])

    for row in range(blocks * trows):
        pl.when(small[1, row // trows, row % trows] > 0)(row_copy(row).start)
    for row in range(blocks * trows):
        pl.when(small[1, row // trows, row % trows] > 0)(row_copy(row).wait)


def list_kernel(small, entries):
    _, blocks, trows = small.shape
    per_row = small.shape[0] - 2
    room = blocks * trows * per_row + GROUP

    ends = (jnp.int32(0),) * len(STAGES)
    for row in range(blocks * trows):
        block, trow = row // trows, row % trows
        live = small[1, block, trow]

        def one(p, ends, row=row, block=block, trow=trow):
            place = small[0, block, small[2 + p, block, trow]]
            entry = place * 512 + (p + (row * per_row + trow * 65536))
            for stage, end in enumerate(ends):
                entries[stage * room + end] = entry
            within = [jnp.where(place < limit, 1, 0) for limit in STAGES[:-1]] + [1]
            return tuple(end + w - v for end, w, v in zip(ends, within, [0] + within[:-1]))

        def some(ends, live=live, one=one):
            return lax.fori_loop(0, live, one, ends)

        ends = lax.cond(live > 0, some, lambda ends: ends, ends)
    for stage, end in enumerate(ends):
        spare = entries[stage * room + jnp.maximum(end - 1, 0)] % 512 + 2 * CHUNKS * 512
        for extra in range(GROUP):
            entries[stage * room + end + extra] = spare
        entries[len(STAGES) * room + stage] = (end + GROUP - 1) // GROUP

def stage_kernel(stage, entries, vals, *refs):
    last = stage == len(STAGES) - 1
    *pieces, out, xs, total = refs if last else refs + (refs[-2],)
    before = pieces.pop(0) if stage else None
    base = STAGES[stage - 1] if stage else 0
    room = vals.shape[0] + GROUP
    rows = 0
    for piece in pieces:
        xs[rows : rows + piece.shape[0], :] = piece[...]
        rows += piece.shape[0]
    xs[rows:, :] = jnp.zeros((TILE, xs.shape[1]), xs.dtype)
    total[...] = jnp.zeros_like(total) if before is None else before[...]

    def step(g, carry):
        products = []
        for k in range(GROUP):
            entry = entries[stage * room + g * GROUP + k]
            place = jnp.minimum(entry // 512 % 128 - base, rows // TILE)
            products.append(
                (
                    pl.multiple_of(entry // 65536 * TILE, TILE),
                    jnp.dot(
                        vals[entry % 512],
                        xs[pl.ds(pl.multiple_of(place * TILE, TILE), TILE), :],
                        preferred_element_type=jnp.float32,
                    ),
                )
            )
        for at, product in products:
            total[pl.ds(at, TILE), :] += product
        return carry

    lax.fori_loop(0, entries[len(STAGES) * room + stage], step, 0)
    if last:
        out[...] = total[...].astype(out.dtype)


def finish_kernel(parts, weight, bias, out):
    total = parts[0].astype(jnp.float32)
    for k in range(1, REPS):
        total = total + parts[k].astype(jnp.float32)
    high = total.astype(jnp.bfloat16)
    low = (total - high.astype(jnp.float32)).astype(jnp.bfloat16)
    hidden = jnp.dot(high, weight[...], preferred_element_type=jnp.float32)
    hidden = hidden + jnp.dot(low, weight[...], preferred_element_type=jnp.float32)
    out[...] = jnp.maximum(hidden + bias[...], 0.0).astype(out.dtype)


SMEM = pl.BlockSpec(memory_space=pltpu.SMEM)
VMEM = pl.BlockSpec(memory_space=pltpu.VMEM)
HBM = pl.BlockSpec(memory_space=pltpu.HBM)


def estimate(flops, moved):
    return pl.CostEstimate(flops=flops, bytes_accessed=moved, transcendentals=0)


def body(features, weight, bias, tile_vals, tile_cols, tile_counts):
    _, blocks, trows, per_row, tile, _ = tile_vals.shape
    tiles = blocks * trows * per_row
    own, feat = features.shape
    device = lax.axis_index("section") * REPS + lax.axis_index("rep")

    def swap(array, pairs):
        return lax.ppermute(array, "section", pairs)

    small = jnp.concatenate(
        [
            lax.dynamic_slice(jnp.asarray(SLOTS), (device, 0, 0), (1, blocks, trows)),
            tile_counts,
            tile_cols[0].transpose(2, 0, 1),
        ],
        0,
    )
    landed = [lax.ppermute(features, ("section", "rep"), pairs) for pairs in LANDS]
    entries = pl.pallas_call(
        list_kernel,
        out_shape=jax.ShapeDtypeStruct((len(STAGES) * (tiles + GROUP + 1),), jnp.int32),
        in_specs=[SMEM],
        out_specs=SMEM,
        compiler_params=pltpu.CompilerParams(vmem_limit_bytes=8 * 2**20),
        cost_estimate=estimate(4000, 4096),
        name="list_live_tiles",
    )(small)
    mine = jnp.concatenate(landed, 0)
    mine, entries, small, vals = lax.optimization_barrier(
        (mine, entries, small, tile_vals.reshape(tiles, tile, tile))
    )

    first = swap(mine, X_SWAPS[0])
    second = swap(mine, X_SWAPS[1])
    vals = pl.pallas_call(
        load_kernel,
        out_shape=jax.ShapeDtypeStruct(vals.shape, vals.dtype),
        in_specs=[SMEM, HBM],
        out_specs=VMEM,
        scratch_shapes=[pltpu.SemaphoreType.DMA((blocks * trows,))],
        compiler_params=pltpu.CompilerParams(vmem_limit_bytes=40 * 2**20),
        cost_estimate=estimate(4000, 4 * vals.size),
        name="load_live_tiles",
    )(small, vals)
    first, vals = lax.optimization_barrier((first, vals))
    third = swap(first, X_SWAPS[1])
    beside = [swap(piece, CORES) for piece in (mine, first, second)]
    def add_stage(stage, before, pieces):
        rows = sum(piece.shape[0] for piece in pieces)
        last = stage == len(STAGES) - 1
        ins = ([before] if stage else []) + list(pieces)
        scratch = [pltpu.VMEM((rows + TILE, feat), jnp.bfloat16)]
        if last:
            scratch.append(pltpu.VMEM((trows * tile, feat), jnp.float32))
        return pl.pallas_call(
            functools.partial(stage_kernel, stage),
            out_shape=jax.ShapeDtypeStruct((trows * tile, feat), jnp.bfloat16 if last else jnp.float32),
            in_specs=[SMEM] + [VMEM] * (1 + len(ins)),
            out_specs=VMEM,
            scratch_shapes=scratch,
            compiler_params=pltpu.CompilerParams(vmem_limit_bytes=24 * 2**20),
            cost_estimate=estimate(2 * rows // 6 * tile * feat, 2**20),
            name=f"sum_stage_{stage}",
        )(entries, vals, *ins)

    acc = add_stage(0, None, (mine, first, second, beside[0]))
    third, acc = lax.optimization_barrier((third, acc))
    final = swap(third, CORES)
    acc = add_stage(1, acc, (third, *beside[1:]))
    final, acc = lax.optimization_barrier((final, acc))
    partial_sums = add_stage(2, acc, (final,))

    parts = lax.all_to_all(partial_sums, "rep", 0, 0, tiled=True)
    return pl.pallas_call(
        finish_kernel,
        out_shape=jax.ShapeDtypeStruct((own, weight.shape[1]), jnp.bfloat16),
        in_specs=[VMEM] * 3,
        out_specs=VMEM,
        compiler_params=pltpu.CompilerParams(vmem_limit_bytes=8 * 2**20),
        cost_estimate=estimate(4 * own * feat * weight.shape[1], 2**20),
        name="apply_weight",
    )(parts.reshape(REPS, own, feat), weight, bias.reshape(1, -1))


def solution(mesh):
    placed = (
        P(("section", "rep"), None),
        P(),
        P(),
        P("section", "rep", None, None, None, None),
        P("section", "rep", None, None),
        P("section", "rep", None),
    )
    return jax.shard_map(
        body, mesh=mesh, in_specs=placed, out_specs=P(("section", "rep"), None), check_vma=False
    )
```

```python
import functools

import jax
import jax.numpy as jnp
import numpy as np
from jax import lax
from jax.experimental import pallas as pl
from jax.experimental.pallas import tpu as pltpu
from jax.sharding import PartitionSpec as P

SECTIONS, REPS, CHUNKS = 32, 8, 32
TILE = 128
STAGES = (32, 56, 64)
GROUP = 8


def section_of(z, x, core):
    return z * 8 + x * 2 + core


def partner(at, odd):
    return (at + 1 - 2 * (at % 2)) % 4 if not odd else (at - 1 + 2 * (at % 2)) % 4


def cheapest(cost):
    n = len(cost)
    rows, columns = [0] * (n + 1), [0] * (n + 1)
    owner, back = [0] * (n + 1), [0] * (n + 1)
    for row in range(1, n + 1):
        owner[0], at = row, 0
        least, used = [float("inf")] * (n + 1), [False] * (n + 1)
        while True:
            used[at] = True
            here = owner[at]
            for j in range(1, n + 1):
                over = cost[here - 1][j - 1] - rows[here] - columns[j]
                if not used[j] and over < least[j]:
                    least[j], back[j] = over, at
            nearest = min((j for j in range(1, n + 1) if not used[j]), key=lambda j: least[j])
            step = least[nearest]
            for j in range(n + 1):
                if used[j]:
                    rows[owner[j]] += step
                    columns[j] -= step
                else:
                    least[j] -= step
            at = nearest
            if owner[at] == 0:
                break
        while at:
            owner[at] = owner[back[at]]
            at = back[at]
    return [owner.index(row, 1) - 1 for row in range(1, n + 1)]


def landings():
    lands = [[], [], [], []]
    spots = [(z, x) for z in range(4) for x in range(4)]
    for owner in range(REPS):
        for core in range(2):
            blocks = range(4 * owner + core, 4 * owner + 4, 2)
            chunks = [(block, replica) for block in blocks for replica in range(REPS)]
            been = [set() for _ in chunks]
            for pairs in lands:
                cost = []
                for (block, replica), planes in zip(chunks, been):
                    beyond = [
                        abs((2 * z + owner // 4 - (block // 8 * 2 + replica // 4) + 4) % 8 - 4)
                        + abs((owner % 4 - replica % 4 + 2) % 4 - 2)
                        + abs((x - block // 2 % 4 + 2) % 4 - 2)
                        for z, x in spots
                    ]
                    cost.append([10**7 if z in planes else hops**8 for (z, _), hops in zip(spots, beyond)])
                for (block, replica), planes, spot in zip(chunks, been, cheapest(cost)):
                    z, x = spots[spot]
                    planes.add(z)
                    pairs.append((block * REPS + replica, section_of(z, x, core) * REPS + owner))
    return lands


def swaps(step):
    pairs = []
    for s in range(SECTIONS):
        z, x, core = s // 8, s // 2 % 4, s % 2
        pairs.append((s, section_of(z, partner(x, (step + core) % 2), core)))
    return pairs


LANDS = landings()
CORES = [(s, s ^ 1) for s in range(SECTIONS)]
X_SWAPS = [swaps(0), swaps(1)]


def chunk_slots():
    def swap(held, pairs):
        got = [None] * len(held)
        for s, t in pairs:
            for r in range(REPS):
                got[t * REPS + r] = held[s * REPS + r]
        return got

    def ring(held, pairs):
        first, second = swap(held, pairs[0]), swap(held, pairs[1])
        return [held, first, second, swap(first, pairs[1])]

    def joined(pieces):
        return [sum(p, []) for p in zip(*pieces)]

    held = [[] for _ in range(SECTIONS * REPS)]
    for pairs in LANDS:
        for source, target in pairs:
            held[target].append(source)
    pieces = ring(held, X_SWAPS)
    beside = [swap(p, CORES) for p in pieces]
    held = joined(pieces[:3] + beside[:1] + pieces[3:] + beside[1:])
    table = np.zeros((SECTIONS * REPS, CHUNKS, 2), np.int32)
    for device in range(SECTIONS * REPS):
        replica = device % REPS
        for place, chunk in enumerate(held[device]):
            table[device, chunk - replica * CHUNKS] = 2 * place, 2 * place + 1
        assert sorted(table[device].ravel()) == list(range(2 * CHUNKS))
    return table.reshape(SECTIONS * REPS, 4, 2 * CHUNKS // 4)


SLOTS = chunk_slots()


def load_kernel(small, tile_vals, vals, sem):
    _, blocks, trows = small.shape
    per_row = small.shape[0] - 2

    def row_copy(row):
        part = pl.ds(row * per_row, per_row)
        return pltpu.make_async_copy(tile_vals.at[part], vals.at[part], sem.at[row])

    for row in range(blocks * trows):
        pl.when(small[1, row // trows, row % trows] > 0)(row_copy(row).start)
    for row in range(blocks * trows):
        pl.when(small[1, row // trows, row % trows] > 0)(row_copy(row).wait)


def list_kernel(small, entries):
    _, blocks, trows = small.shape
    per_row = small.shape[0] - 2
    room = blocks * trows * per_row + GROUP

    ends = (jnp.int32(0),) * len(STAGES)
    for row in range(blocks * trows):
        block, trow = row // trows, row % trows
        live = small[1, block, trow]

        def one(p, ends, row=row, block=block, trow=trow):
            place = small[0, block, small[2 + p, block, trow]]
            entry = place * 512 + (p + (row * per_row + trow * 65536))
            for stage, end in enumerate(ends):
                entries[stage * room + end] = entry
            within = [jnp.where(place < limit, 1, 0) for limit in STAGES[:-1]] + [1]
            return tuple(end + w - v for end, w, v in zip(ends, within, [0] + within[:-1]))

        def some(ends, live=live, one=one):
            return lax.fori_loop(0, live, one, ends)

        ends = lax.cond(live > 0, some, lambda ends: ends, ends)
    for stage, end in enumerate(ends):
        spare = entries[stage * room + jnp.maximum(end - 1, 0)] % 512 + 2 * CHUNKS * 512
        for extra in range(GROUP):
            entries[stage * room + end + extra] = spare
        entries[len(STAGES) * room + stage] = (end + GROUP - 1) // GROUP

def stage_kernel(stage, entries, vals, *refs):
    last = stage == len(STAGES) - 1
    *pieces, out, xs, total = refs if last else refs + (refs[-2],)
    before = pieces.pop(0) if stage else None
    base = STAGES[stage - 1] if stage else 0
    room = vals.shape[0] + GROUP
    rows = 0
    for piece in pieces:
        xs[rows : rows + piece.shape[0], :] = piece[...]
        rows += piece.shape[0]
    xs[rows:, :] = jnp.zeros((TILE, xs.shape[1]), xs.dtype)
    total[...] = jnp.zeros_like(total) if before is None else before[...]

    def step(g, carry):
        products = []
        for k in range(GROUP):
            entry = entries[stage * room + g * GROUP + k]
            place = jnp.minimum(entry // 512 % 128 - base, rows // TILE)
            products.append(
                (
                    pl.multiple_of(entry // 65536 * TILE, TILE),
                    jnp.dot(
                        vals[entry % 512],
                        xs[pl.ds(pl.multiple_of(place * TILE, TILE), TILE), :],
                        preferred_element_type=jnp.float32,
                    ),
                )
            )
        for at, product in products:
            total[pl.ds(at, TILE), :] += product
        return carry

    lax.fori_loop(0, entries[len(STAGES) * room + stage], step, 0)
    if last:
        out[...] = total[...].astype(out.dtype)


def finish_kernel(parts, weight, bias, out):
    total = parts[0].astype(jnp.float32)
    for k in range(1, REPS):
        total = total + parts[k].astype(jnp.float32)
    high = total.astype(jnp.bfloat16)
    low = (total - high.astype(jnp.float32)).astype(jnp.bfloat16)
    hidden = jnp.dot(high, weight[...], preferred_element_type=jnp.float32)
    hidden = hidden + jnp.dot(low, weight[...], preferred_element_type=jnp.float32)
    out[...] = jnp.maximum(hidden + bias[...], 0.0).astype(out.dtype)


SMEM = pl.BlockSpec(memory_space=pltpu.SMEM)
VMEM = pl.BlockSpec(memory_space=pltpu.VMEM)
HBM = pl.BlockSpec(memory_space=pltpu.HBM)


def estimate(flops, moved):
    return pl.CostEstimate(flops=flops, bytes_accessed=moved, transcendentals=0)


def body(features, weight, bias, tile_vals, tile_cols, tile_counts):
    _, blocks, trows, per_row, tile, _ = tile_vals.shape
    tiles = blocks * trows * per_row
    own, feat = features.shape
    device = lax.axis_index("section") * REPS + lax.axis_index("rep")

    def swap(array, pairs):
        return lax.ppermute(array, "section", pairs)

    small = jnp.concatenate(
        [
            lax.dynamic_slice(jnp.asarray(SLOTS), (device, 0, 0), (1, blocks, trows)),
            tile_counts,
            tile_cols[0].transpose(2, 0, 1),
        ],
        0,
    )
    landed = [lax.ppermute(features, ("section", "rep"), pairs) for pairs in LANDS]
    entries = pl.pallas_call(
        list_kernel,
        out_shape=jax.ShapeDtypeStruct((len(STAGES) * (tiles + GROUP + 1),), jnp.int32),
        in_specs=[SMEM],
        out_specs=SMEM,
        compiler_params=pltpu.CompilerParams(vmem_limit_bytes=8 * 2**20),
        cost_estimate=estimate(4000, 4096),
        name="list_live_tiles",
    )(small)
    mine = jnp.concatenate(landed, 0)
    mine, entries, small, vals = lax.optimization_barrier(
        (mine, entries, small, tile_vals.reshape(tiles, tile, tile))
    )

    first = swap(mine, X_SWAPS[0])
    second = swap(mine, X_SWAPS[1])
    vals = pl.pallas_call(
        load_kernel,
        out_shape=jax.ShapeDtypeStruct(vals.shape, vals.dtype),
        in_specs=[SMEM, HBM],
        out_specs=VMEM,
        scratch_shapes=[pltpu.SemaphoreType.DMA((blocks * trows,))],
        compiler_params=pltpu.CompilerParams(vmem_limit_bytes=40 * 2**20),
        cost_estimate=estimate(4000, 4 * vals.size),
        name="load_live_tiles",
    )(small, vals)
    first, vals = lax.optimization_barrier((first, vals))
    third = swap(first, X_SWAPS[1])
    beside = [swap(piece, CORES) for piece in (mine, first, second)]
    def add_stage(stage, before, pieces):
        rows = sum(piece.shape[0] for piece in pieces)
        last = stage == len(STAGES) - 1
        ins = ([before] if stage else []) + list(pieces)
        scratch = [pltpu.VMEM((rows + TILE, feat), jnp.bfloat16)]
        if last:
            scratch.append(pltpu.VMEM((trows * tile, feat), jnp.float32))
        return pl.pallas_call(
            functools.partial(stage_kernel, stage),
            out_shape=jax.ShapeDtypeStruct((trows * tile, feat), jnp.bfloat16 if last else jnp.float32),
            in_specs=[SMEM] + [VMEM] * (1 + len(ins)),
            out_specs=VMEM,
            scratch_shapes=scratch,
            compiler_params=pltpu.CompilerParams(vmem_limit_bytes=24 * 2**20),
            cost_estimate=estimate(2 * rows // 6 * tile * feat, 2**20),
            name=f"sum_stage_{stage}",
        )(entries, vals, *ins)

    acc = add_stage(0, None, (mine, first, second, beside[0]))
    third, acc = lax.optimization_barrier((third, acc))
    final = swap(third, CORES)
    acc = add_stage(1, acc, (third, *beside[1:]))
    final, acc = lax.optimization_barrier((final, acc))
    partial_sums = add_stage(2, acc, (final,))

    parts = lax.all_to_all(partial_sums, "rep", 0, 0, tiled=True)
    return pl.pallas_call(
        finish_kernel,
        out_shape=jax.ShapeDtypeStruct((own, weight.shape[1]), jnp.bfloat16),
        in_specs=[VMEM] * 3,
        out_specs=VMEM,
        compiler_params=pltpu.CompilerParams(vmem_limit_bytes=8 * 2**20),
        cost_estimate=estimate(4 * own * feat * weight.shape[1], 2**20),
        name="apply_weight",
    )(parts.reshape(REPS, own, feat), weight, bias.reshape(1, -1))


def solution(mesh):
    placed = (
        P(("section", "rep"), None),
        P(),
        P(),
        P("section", "rep", None, None, None, None),
        P("section", "rep", None, None),
        P("section", "rep", None),
    )
    return jax.shard_map(
        body, mesh=mesh, in_specs=placed, out_specs=P(("section", "rep"), None), check_vma=False
    )
```
